128 devices in a mesh: row: 8 (over x, y_hi), col: 16 (over z, y_lo, core).
Axes of the slice: x: 4, y: 4 (y_hi: 2, y_lo: 2; y = y_hi * 2 + y_lo), z: 4, core: 2. Of those that a mesh axis runs over, the one named last changes fastest.
Arguments:
- amplitudes: bfloat16 [240, 240, 1024], P('row', None, 'col'), may hold values from -6 to 6
- pp_integrals: bfloat16 [1024, 1024], P('row', 'col'), may hold values from -0.1875 to 0.1875
- cycle_integrals: bfloat16 [240, 32, 7680], P('row', None, 'col'), may hold values from -0.0625 to 0.0625
- occ_map: int32 [8, 8], replicated, may hold values 0 or 1
- vir_map: int32 [16, 16], replicated, may hold values 0 or 1
Outputs:
- ladder: bfloat16 [240, 240, 1024], P('row', None, 'col')
- cycle_out: bfloat16 [240, 32, 7680], P('row', None, 'col')
The draws below stay inside these ranges and needn't reach their ends.
All inputs are finite; a program needn't handle non-finite values.
Results may differ from the reference program's by a relative error of at most 0.001.
Values may be sent and summed in bfloat16 or wider, within the bound.
No kernel may reach another device: no remote copies, remote signals or barrier semaphores. Data moves between devices by JAX's collectives and lax.ppermute only.
A program may use at most 128 MiB of HBM per device.

```python
import jax
import jax.numpy as jnp

O = 240
VA_DEV = 2
OTILES = 8
NA = 32
N_COL = 16


def with_ends(drawn, rng, low, high):
    spot = [jax.random.randint(jax.random.fold_in(rng, axis), (), 0, length) for axis, length in enumerate(drawn.shape)]
    main_axis = drawn.shape.index(max(drawn.shape))
    next_to = spot[:main_axis] + [(spot[main_axis] + 1) % drawn.shape[main_axis]] + spot[main_axis + 1:]
    return drawn.at[tuple(spot)].set(low).at[tuple(next_to)].set(high)


def block_scale(key, dims, split, least, high):
    loudness, own = 1.0, jax.random.fold_in(key, 6)
    for position, shards_of in split:
        steps = jnp.exp(jax.random.uniform(jax.random.fold_in(own, position), (shards_of,), jnp.float32, least / len(split), high / len(split)))
        loudness = loudness * jnp.repeat(steps, dims[position] // shards_of).reshape([-1 if axis == position else 1 for axis in range(len(dims))])
    return loudness


def normal_values(own_key, shape, deviation, limit, shards=(), dtype=jnp.bfloat16):
    result = jax.random.normal(own_key, shape, jnp.float32) * deviation
    if len(shards) > 0:
        result = block_scale(own_key, shape, shards, -0.22, 0.18) * result
    return jnp.clip(result, min=-limit, max=limit).astype(dtype)


def setup_inputs(seed: int = 0) -> dict:
    streams_of = jax.random.split(jax.random.key(seed), 6)
    amplitudes = normal_values(streams_of[0], (O, O, NA * NA), 1.0, 6.0, ((0, 8), (2, 16)))
    pp_integrals = normal_values(streams_of[1], (NA * NA, NA * NA), (NA * NA) ** -0.5, 0.1875, ((0, 8), (1, 16)))
    cycle_integrals = normal_values(streams_of[2], (O, NA, O * NA), (O * NA) ** -0.5, 0.0625, ((0, 8), (2, 16)))
    occ_map = with_ends((jax.random.randint(streams_of[3], (OTILES, OTILES), 0, 4) < 3).astype(jnp.int32), jax.random.fold_in(streams_of[3], 1), 0, 1)
    vir_map = with_ends((jax.random.randint(streams_of[4], (N_COL, N_COL), 0, 4) < 3).astype(jnp.int32), jax.random.fold_in(streams_of[4], 1), 0, 1)
    return {"amplitudes": amplitudes, "pp_integrals": pp_integrals, "cycle_integrals": cycle_integrals, "occ_map": occ_map, "vir_map": vir_map}


def reference(amplitudes, pp_integrals, cycle_integrals, occ_map, vir_map):
    tile_size = O // OTILES
    occ_full = jnp.repeat(jnp.repeat(occ_map, tile_size, axis=0), tile_size, axis=1)
    vir_full = jnp.repeat(jnp.repeat(vir_map, VA_DEV, axis=0), VA_DEV, axis=1)
    mask = (occ_full[:, :, None] * vir_full.reshape(1, 1, NA * NA)).astype(jnp.bfloat16)
    masked = amplitudes * mask
    ladder = jnp.dot(masked.reshape(O * O, NA * NA), pp_integrals, preferred_element_type=jnp.float32)
    ladder = ladder.astype(jnp.bfloat16).reshape(O, O, NA * NA)
    relaid = masked.reshape(O, O, NA, NA).transpose(0, 2, 1, 3).reshape(O * NA, O * NA)
    cycle_out = jnp.dot(relaid, cycle_integrals.reshape(O * NA, O * NA), preferred_element_type=jnp.float32)
    cycle_out = cycle_out.astype(jnp.bfloat16).reshape(O, NA, O * NA)
    return ladder, cycle_out
```

```python
import jax
import jax.numpy as jnp
from jax import lax
from jax.experimental import pallas as pl
from jax.experimental.pallas import tpu as pltpu
from jax.sharding import PartitionSpec as P

BF = jnp.bfloat16
F32 = jnp.float32
VMEM_LIMIT = 60 * 1024 * 1024
GROUP = 8


def dot(a, b):
    return jnp.dot(a, b, preferred_element_type=F32)


def iota(shape, dim):
    return lax.broadcasted_iota(jnp.int32, shape, dim)


def slot_rows(row):
    x, yh = row // 2, row % 2
    return [((x + dx) % 4) * 2 + (yh + dy) % 2 for dy in (0, 1) for dx in (0, 3, 1, 2)]


def slot_of(row, other):
    dx = (other // 2 - row // 2 + 4) % 4
    base = jnp.where(dx == 0, 0, jnp.where(dx == 3, 1, jnp.where(dx == 1, 2, 3)))
    return base + 4 * ((other + row) % 2)


def piece_ids(col):
    z, yl, core = col // 4, (col // 2) % 2, col % 2
    e = 2 * core - 1
    ids = []
    for dy in (0, 1):
        y = (yl + dy) % 2
        for dz, dc in ((0, 0), (0, 1), (e, 0), (e, 1), (2, 0), (-e, 1), (-e, 0), (2, 1)):
            ids.append(((z + dz + 4) % 4) * 4 + y * 2 + (core + dc) % 2)
    return ids


def lane_map(row, shape, dim):
    lane = iota(shape, dim)
    block, t = lane // 32, lane % 32
    start = jnp.zeros(shape, jnp.int32)
    for k, r in enumerate(slot_rows(row)):
        start = jnp.where(block == k, r * 30, start)
    return start + t, t < 30, block


def prepare_kernel(occ_ref, vir_ref, amp_ref, cyc_ref, pp_ref, a_out, b_out):
    row, col = lax.axis_index("row"), lax.axis_index("col")
    source, held, block = lane_map(row, (1, 256), 1)
    keep = jnp.zeros((1, 256), jnp.int32)
    for k, r in enumerate(slot_rows(row)):
        keep = jnp.where(block == k, occ_ref[row, r], keep)
    keep = jnp.where(held, keep, 0)
    place = jnp.where(iota((240, 256), 0) == source, keep, 0).astype(F32).astype(BF)
    pair = (iota((64, 256), 0) % 32) // 2
    vir = jnp.zeros((64, 256), jnp.int32)
    for k in range(16):
        vir = jnp.where(pair == k, vir_ref[col, k], vir)
    vir = vir.astype(F32)

    def step(i, _):
        a_out[pl.ds(pl.multiple_of(i * 64, 64), 64), :] = (dot(amp_ref[i], place) * vir).astype(BF)
        return 0

    lax.fori_loop(0, 30, step, 0, unroll=5)
    b_out[:, 0:480] = cyc_ref[...]
    for part in range(4):
        b_out[pl.ds(part * 64, 64), 480:512] = pp_ref[:, part * 32:(part + 1) * 32]
    b_out[256:960, 480:512] = jnp.zeros((704, 32), BF)


def prepare(occ_map, vir_map, amp_t, cyc, pp_t):
    return pl.pallas_call(
        prepare_kernel,
        out_shape=(jax.ShapeDtypeStruct((1920, 256), BF), jax.ShapeDtypeStruct((960, 512), BF)),
        in_specs=[pl.BlockSpec(memory_space=pltpu.SMEM)] * 2 + [pl.BlockSpec(memory_space=pltpu.VMEM)] * 3,
        out_specs=(pl.BlockSpec(memory_space=pltpu.VMEM),) * 2,
        compiler_params=pltpu.CompilerParams(vmem_limit_bytes=VMEM_LIMIT),
        cost_estimate=pl.CostEstimate(flops=2 * 1920 * 256 * 256, bytes_accessed=4000000, transcendentals=0),
        name="prepare",
    )(occ_map, vir_map, amp_t, cyc, pp_t)


def regroup_matrix():
    o, s = iota((256, 256), 0), iota((256, 256), 1)
    return jnp.where((s % 32 == o // 8) & (s // 32 == o % 8), 1.0, 0.0).astype(BF)


def regroup(perm, source, count, width):
    for first in range(0, count, 16):
        halves = []
        for m in (first, first + 8):
            n = min(count - m, 8) * 32
            halves.append(dot(perm[:, 0:n], source[pl.ds(m * 32, n), :]).reshape(32, 8, width))
        yield first, jnp.concatenate(halves, axis=1).astype(BF)


def product_kernel(*refs):
    a_refs, b_refs = refs[:16], refs[16:24]
    lad_ref, cyc_ref = refs[24:26]
    a_nat, b_nat, a_cyc, b_cyc, c_out, lad, a_sem, b_sem = refs[26:]
    row, col = lax.axis_index("row"), lax.axis_index("col")
    core = col % 2
    b_copies = [pltpu.make_async_copy(b_refs[k], b_nat.at[k], b_sem.at[k]) for k in range(8)]
    a_copies = [pltpu.make_async_copy(a_refs[k], a_nat.at[k], a_sem.at[k]) for k in range(16)]
    for copy in b_copies + a_copies:
        copy.start()
    perm = regroup_matrix()
    slots = [0, 1 + core, 2 - core, 3]
    slots = slots + [s + 4 for s in slots]
    for k in range(8):
        b_copies[k].wait()
        base = slots[k] * 32
        for first, part in regroup(perm, b_nat.at[k], 30, 512):
            b_cyc[:, pl.ds(pl.multiple_of(base + first, 16), 16), :] = part
    ids = piece_ids(col)
    for group in range(2):
        pieces = range(group * GROUP, (group + 1) * GROUP)
        for n, k in enumerate(pieces):
            a_copies[k].wait()
            for first, part in regroup(perm, a_nat.at[k], 60, 256):
                a_cyc[:, pl.ds(n * 64 + first, 16), :] = part
        for c in range(0, 32, 8):
            left = jnp.concatenate([a_cyc[c + d] for d in range(8)], axis=1)
            right = b_cyc[pl.ds(c, 8), :, :].reshape(2048, 512)
            if c == 0:
                c_acc = dot(left, right)
            else:
                c_acc = c_acc + dot(left, right)
        c_out[pl.ds(group * 512, 512), :] = c_acc.astype(BF)
        tiles = []
        for pair in range(GROUP // 2):
            tile = jnp.zeros((64, 128), F32)
            for half in range(2):
                p = ids[group * GROUP + pair * 2 + half]
                slot = slot_of(row, p // 2)
                place = jnp.where(slot % 4 == 1, 1 + core, jnp.where(slot % 4 == 2, 2 - core, slot % 4)) + 4 * (slot // 4)
                for a in range(2):
                    at = pl.multiple_of((p % 2) * 128 + a * 64, 64)
                    values = b_nat[place, pl.ds(at, 64), 384:512]
                    s, d = iota((128, 128), 0), iota((128, 128), 1)
                    move = jnp.where((s >= 96) & (d == s - 96 + half * 64 + a * 32), 1.0, 0.0).astype(BF)
                    tile = tile + dot(values, move)
            tiles.append(tile.astype(BF))
        v_left = jnp.concatenate(tiles, axis=1)

        def ladder_step(i, _):
            at = pl.ds(pl.multiple_of(i * 64, 64), 64)
            right = jnp.concatenate([a_nat[k, at, :] for k in pieces], axis=0)
            value = dot(v_left, right)
            if group == 0:
                lad[at, :] = value
            else:
                lad[at, :] = lad[at, :] + value
            return 0

        lax.fori_loop(0, 30, ladder_step, 0, unroll=3)
    source, held, _ = lane_map(row, (256, 1), 0)
    back = jnp.where((iota((256, 240), 1) == source) & held, 1.0, 0.0).astype(BF)
    lad_ref[...] = dot(lad[...].astype(BF), back).astype(BF)
    o, s = iota((256, 256), 0), iota((256, 256), 1)
    target = jnp.zeros((256, 256), jnp.int32)
    for k in range(16):
        target = jnp.where(s // 16 == k, ids[k], target)
    target = ((s % 16) // 2) * 32 + target * 2 + s % 2
    spread = jnp.where(o == target, 1.0, 0.0).astype(BF)
    for g in range(4):
        block = jnp.concatenate([c_out[pl.ds(k * 64 + g * 16, 16), :] for k in range(16)], axis=0)
        n = 256 if g < 3 else 192
        cyc_ref[pl.ds(g * 256, n), :] = dot(spread[0:n], block)[:, 0:480].astype(BF)


def products(a_pieces, b_pieces):
    return pl.pallas_call(
        product_kernel,
        out_shape=(jax.ShapeDtypeStruct((1920, 240), BF), jax.ShapeDtypeStruct((960, 480), BF)),
        in_specs=[pl.BlockSpec(memory_space=pl.ANY)] * 24,
        out_specs=(pl.BlockSpec(memory_space=pltpu.VMEM),) * 2,
        scratch_shapes=[
            pltpu.VMEM((16, 1920, 256), BF),
            pltpu.VMEM((8, 960, 512), BF),
            pltpu.VMEM((32, GROUP * 64, 256), BF),
            pltpu.VMEM((32, 256, 512), BF),
            pltpu.VMEM((1024, 512), BF),
            pltpu.VMEM((1920, 256), F32),
            pltpu.SemaphoreType.DMA((16,)),
            pltpu.SemaphoreType.DMA((8,)),
        ],
        compiler_params=pltpu.CompilerParams(vmem_limit_bytes=VMEM_LIMIT),
        cost_estimate=pl.CostEstimate(flops=20 * 10**9, bytes_accessed=26 * 10**6, transcendentals=0),
        name="products",
    )(*a_pieces, *b_pieces)


def permute(value, move):
    pairs = []
    for row in range(8):
        for col in range(16):
            here = (row // 2, (row % 2) * 2 + (col // 2) % 2, col // 4, col % 2)
            x, y, z, core = move(*here)
            x, y, z = x % 4, y % 4, z % 4
            pairs.append((row * 16 + col, (x * 2 + y // 2) * 16 + z * 4 + (y % 2) * 2 + core))
    return lax.ppermute(value, ("row", "col"), pairs)


def along_z(value):
    return permute(value, lambda x, y, z, c: (x, y, z + 1 - 2 * c, c))


def along_x(value):
    return permute(value, lambda x, y, z, c: (x + 1 - 2 * c, y, z, c))


def swap(value):
    return permute(value, lambda x, y, z, c: (x, y, z, 1 - c))


def near_y(value):
    return permute(value, lambda x, y, z, c: (x, y ^ 1, z, c))


def far_y(value):
    return permute(value, lambda x, y, z, c: (x, y + 2, z, c))


def gather_a(own):
    other = swap(own)
    c1, c2 = along_z(own), along_z(other)
    c5 = along_z(c1)
    return [own, other, c1, c2, c5, swap(c1), swap(c2), swap(c5)]


def gather_b(own):
    other = swap(own)
    d1, d2 = along_x(own), along_x(other)
    d5 = along_x(d1)
    return [own, d1, swap(d2), d5]


def on_device(amplitudes, pp_integrals, cycle_integrals, occ_map, vir_map):
    amp_t = jnp.transpose(amplitudes, (0, 2, 1))
    a, b = prepare(occ_map, vir_map, amp_t, cycle_integrals.reshape(960, 480), pp_integrals.T)
    bq = far_y(b)
    aq = near_y(a)
    a_pieces = gather_a(a) + gather_a(aq)
    b_pieces = gather_b(b) + gather_b(bq)
    ladder, cycle_out = products(a_pieces, b_pieces)
    ladder = jnp.transpose(ladder.reshape(30, 64, 240), (0, 2, 1))
    return ladder, cycle_out.reshape(30, 32, 480)


def solution(mesh):
    in_specs = (P("row", None, "col"), P("row", "col"), P("row", None, "col"), P(), P())
    out_specs = (P("row", None, "col"), P("row", None, "col"))
    return jax.shard_map(
        on_device, mesh=mesh, in_specs=in_specs, out_specs=out_specs, check_vma=False
    )
```

```python
import functools

import jax
import jax.numpy as jnp
from jax import lax
from jax.experimental import pallas as pl
from jax.experimental.pallas import tpu as pltpu
from jax.sharding import PartitionSpec as P

BF = jnp.bfloat16
F32 = jnp.float32
PARAMS = pltpu.CompilerParams(vmem_limit_bytes=56 * 1024 * 1024)
VMEM = pl.BlockSpec(memory_space=pltpu.VMEM)
SMEM = pl.BlockSpec(memory_space=pltpu.SMEM)
ANY = pl.BlockSpec(memory_space=pl.ANY)


def cost(flops, size):
    return pl.CostEstimate(flops=flops, bytes_accessed=size, transcendentals=0)


def dot(a, b):
    return jnp.dot(a, b, preferred_element_type=F32)


def iota(shape, dim):
    return lax.broadcasted_iota(jnp.int32, shape, dim)


def here():
    return lax.axis_index("row"), lax.axis_index("col")


def slot_rows(row):
    x, yh = row // 2, row % 2
    return [((x + dx) % 4) * 2 + (yh + dy) % 2 for dy in (0, 1) for dx in (0, 3, 1, 2)]


def piece_ids(col):
    z, yl, core = col // 4, (col // 2) % 2, col % 2
    e = 2 * core - 1
    near = dict(a=(0, 0), s_a=(0, 1), c1=(e, 0), c2=(e, 1), c5=(2, 0), s_c1=(-e, 1), s_c2=(-e, 0), s_c5=(2, 1))
    far = dict(aq="a", s_aq="s_a", cq1="c1", cq2="c2", cq5="c5", s_cq1="s_c1", s_cq2="s_c2", s_cq5="s_c5")
    ids = {}
    for dy in (0, 1):
        for name in far if dy else near:
            dz, dc = near[far[name] if dy else name]
            ids[name] = ((z + dz + 4) % 4) * 4 + ((yl + dy) % 2) * 2 + (core + dc) % 2
    return ids


def lane_map(row, shape, dim):
    lane = iota(shape, dim)
    block, t = lane // 32, lane % 32
    start = jnp.zeros(shape, jnp.int32)
    for k, r in enumerate(slot_rows(row)):
        start = jnp.where(block == k, r * 30, start)
    return start + t, t < 30, block


def prepare_kernel(occ_ref, vir_ref, amp_ref, out_ref, place_ref, vir_rows_ref):
    row, col = here()

    @pl.when(pl.program_id(0) == 0)
    def _():
        source, held, block = lane_map(row, (1, 256), 1)
        keep = jnp.zeros((1, 256), jnp.int32)
        for k, r in enumerate(slot_rows(row)):
            keep = jnp.where(block == k, occ_ref[row, r], keep)
        keep = jnp.where(held, keep, 0)
        place_ref[...] = jnp.where(iota((240, 256), 0) == source, keep, 0).astype(F32).astype(BF)
        pair = (iota((64, 256), 0) % 32) // 2
        vir = jnp.zeros((64, 256), jnp.int32)
        for k in range(16):
            vir = jnp.where(pair == k, vir_ref[col, k], vir)
        vir_rows_ref[...] = vir.astype(F32)

    value = dot(amp_ref[...], place_ref[...])
    value = value.reshape(6, 64, 256) * vir_rows_ref[...][None]
    out_ref[...] = value.reshape(384, 256).astype(BF)


def prepare(occ_map, vir_map, amp):
    return pl.pallas_call(
        prepare_kernel,
        grid=(5,),
        out_shape=jax.ShapeDtypeStruct((1920, 256), BF),
        in_specs=[SMEM, SMEM, pl.BlockSpec((384, 240), lambda i: (i, 0))],
        out_specs=pl.BlockSpec((384, 256), lambda i: (i, 0)),
        scratch_shapes=[pltpu.VMEM((240, 256), BF), pltpu.VMEM((64, 256), F32)],
        compiler_params=PARAMS,
        cost_estimate=cost(2 * 1920 * 256 * 256, 2000000),
        name="prepare",
    )(occ_map, vir_map, amp)


def regroup_matrix():
    o, s = iota((256, 256), 0), iota((256, 256), 1)
    return jnp.where((s % 32 == o // 8) & (s // 32 == o % 8), 1.0, 0.0).astype(BF)


def regroup(perm, source, count, width):
    for first in range(0, count, 16):
        halves = []
        for m in (first, first + 8):
            n = min(count - m, 8) * 32
            halves.append(dot(perm[:, 0:n], source[pl.ds(m * 32, n), :]).reshape(32, 8, width))
        yield first, jnp.concatenate(halves, axis=1).astype(BF)


def prepare_b_kernel(cyc_ref, pp_ref, out_ref):
    for first, part in regroup(regroup_matrix(), cyc_ref, 30, 480):
        out_ref[:, pl.ds(first, 16), 0:480] = part
    for q in range(4):
        out_ref[pl.ds(2 * q, 2), :, 480:512] = pp_ref[:, q * 32:(q + 1) * 32].reshape(2, 32, 32)
    out_ref[8:32, :, 480:512] = jnp.zeros((24, 32, 32), BF)


def prepare_b(cyc, pp_t):
    return pl.pallas_call(
        prepare_b_kernel,
        out_shape=jax.ShapeDtypeStruct((32, 32, 512), BF),
        in_specs=[VMEM] * 2,
        out_specs=VMEM,
        compiler_params=PARAMS,
        cost_estimate=cost(2 * 10**8, 2 * 10**6),
        name="prepare_b",
    )(cyc, pp_t)


def slot_of(row, other):
    dx = (other // 2 - row // 2 + 4) % 4
    base = jnp.where(dx == 0, 0, jnp.where(dx == 3, 1, jnp.where(dx == 1, 2, 3)))
    return base + 4 * ((other + row) % 2)


def fetch_b(pieces, vmem, sems, col):
    core = col % 2
    copies = []
    for k, place in enumerate((0, 1 + core, 2 - core, 3)):
        at = pl.ds(pl.multiple_of(place * 32, 32), 32)
        copies.append(pltpu.make_async_copy(pieces[k], vmem.at[:, at, :], sems.at[k]))
        copies[-1].start()
    return copies


def cycle_product(left, right, lanes, start=None):
    total = start
    step = 2048 // (lanes[1] - lanes[0])
    for c in range(0, 32, step):
        l = jnp.concatenate([left(c + d)[:, lanes[0]:lanes[1]] for d in range(step)], axis=1)
        r = right[pl.ds(c, step), :, :].reshape(2048, 512)
        value = dot(l, r)
        total = value if total is None else total + value
    return total


def ladder_weights(v_ref, row, ids):
    s, d = iota((128, 128), 0), iota((128, 128), 1)
    tiles = []
    for pair in range(0, len(ids), 2):
        tile = jnp.zeros((64, 128), F32)
        for half in range(2):
            p = ids[pair + half]
            slot = slot_of(row, p // 2)
            for a in range(2):
                values = v_ref[slot, pl.ds((p % 2) * 4 + a * 2, 2), :, :].reshape(64, 128)
                move = jnp.where((s >= 96) & (d == s - 96 + half * 64 + a * 32), 1.0, 0.0).astype(BF)
                tile = tile + dot(values, move)
        tiles.append(tile.astype(BF))
    return jnp.concatenate(tiles, axis=1)


def ladder_product(weights, pieces, start, out):
    def step(i, _):
        at = pl.ds(pl.multiple_of(i * 64, 64), 64)
        right = jnp.concatenate([p[at, :] for p in pieces], axis=0)
        value = dot(weights, right)
        out[at, :] = value if start is None else value + start[at, :]
        return 0

    lax.fori_loop(0, 30, step, 0, unroll=5)


def partial_kernel(*refs):
    pieces, b_refs, (late_ref, acc_ref, a_ref, b_vmem, sems) = refs[:4], refs[4:8], refs[8:]
    _, col = here()
    copies = fetch_b(b_refs, b_vmem, sems, col)
    perm = regroup_matrix()
    for n, piece in enumerate(pieces):
        for m, part in regroup(perm, piece, 60, 256):
            a_ref[:, pl.ds(n * 64 + m, 16), :] = part[:, :, 0:128]
            late_ref[:, pl.ds(n * 64 + m, 16), :] = part[:, :, 128:256]
    for copy in copies:
        copy.wait()
    acc_ref[...] = cycle_product(lambda c: a_ref[c], b_vmem, (0, 128))


def partial_products(name, pieces, b_early):
    return pl.pallas_call(
        partial_kernel,
        out_shape=(jax.ShapeDtypeStruct((32, 256, 128), BF), jax.ShapeDtypeStruct((256, 512), F32)),
        in_specs=[VMEM] * 4 + [ANY] * 4,
        out_specs=(VMEM,) * 2,
        scratch_shapes=[
            pltpu.VMEM((32, 256, 128), BF),
            pltpu.VMEM((32, 128, 512), BF),
            pltpu.SemaphoreType.DMA((4,)),
        ],
        compiler_params=PARAMS,
        cost_estimate=cost(3 * 10**9, 12 * 10**6),
        name="partial_" + name,
    )(*pieces, *b_early)


def ladder_kernel(names, *refs):
    count = len(names)
    pieces, b_refs, (out_ref, a_vmem, v_vmem, a_sems, v_sems) = refs[:count], refs[count:count + 8], refs[count + 8:]
    row, col = here()
    core = col % 2
    slots = [0, 1 + core, 2 - core, 3, 4, 5 + core, 6 - core, 7]
    v_copies = [
        pltpu.make_async_copy(b_refs[k].at[0:8, :, 384:512], v_vmem.at[slots[k]], v_sems.at[k]) for k in range(8)
    ]
    a_copies = [pltpu.make_async_copy(pieces[k], a_vmem.at[k], a_sems.at[k]) for k in range(count)]
    for copy in v_copies + a_copies:
        copy.start()
    for copy in v_copies:
        copy.wait()
    ids = piece_ids(col)
    for first in range(0, count, 4):
        for k in range(first, first + 4):
            a_copies[k].wait()
        weights = ladder_weights(v_vmem, row, [ids[n] for n in names[first:first + 4]])
        parts = [a_vmem.at[k] for k in range(first, first + 4)]
        ladder_product(weights, parts, None if first == 0 else out_ref, out_ref)


def ladder_part(names, pieces, b_all):
    count = len(names)
    return pl.pallas_call(
        functools.partial(ladder_kernel, names),
        out_shape=jax.ShapeDtypeStruct((1920, 256), F32),
        in_specs=[ANY] * (count + 8),
        out_specs=VMEM,
        scratch_shapes=[
            pltpu.VMEM((count, 1920, 256), BF),
            pltpu.VMEM((8, 8, 32, 128), BF),
            pltpu.SemaphoreType.DMA((count,)),
            pltpu.SemaphoreType.DMA((8,)),
        ],
        compiler_params=PARAMS,
        cost_estimate=cost(3 * 10**9, 14 * 10**6),
        name="ladder_part",
    )(*pieces, *b_all)


def last_kernel(names, *refs):
    refs = list(refs)

    def take(n):
        out = refs[:n]
        del refs[:n]
        return out

    pieces, b_refs, lates, accs, (lad_in,) = take(4), take(8), take(3), take(3), take(1)
    lad_out, cyc_out = take(2)
    a_ref, b_early, b_late, v_vmem, late_vmem, c_ref, lad_ref, sems, b_sems, v_sems = refs
    row, col = here()
    core = col % 2
    late_copies = fetch_b(b_refs[4:8], b_late, b_sems.at[1], col)
    copies = [pltpu.make_async_copy(lates[k], late_vmem.at[k], sems.at[k]) for k in range(3)]
    for copy in copies:
        copy.start()
    early_copies = fetch_b(b_refs[0:4], b_early, b_sems.at[0], col)
    slots = [0, 1 + core, 2 - core, 3, 4, 5 + core, 6 - core, 7]
    v_copies = [
        pltpu.make_async_copy(b_refs[k].at[0:8, :, 384:512], v_vmem.at[slots[k]], v_sems.at[k]) for k in range(8)
    ]
    for copy in v_copies:
        copy.start()
    ids = piece_ids(col)
    perm = regroup_matrix()
    for n, piece in enumerate(pieces):
        for m, part in regroup(perm, piece, 60, 256):
            a_ref[:, pl.ds(n * 64 + m, 16), :] = part
    for copy in late_copies:
        copy.wait()
    for k in range(3):
        copies[k].wait()
        total = cycle_product(lambda c: late_vmem[k, c], b_late, (0, 128), accs[k][...])
        c_ref[pl.ds(k * 256, 256), :] = total.astype(BF)
    total = cycle_product(lambda c: a_ref[c], b_late, (128, 256))
    for copy in early_copies:
        copy.wait()
    total = cycle_product(lambda c: a_ref[c], b_early, (0, 128), total)
    c_ref[pl.ds(768, 256), :] = total.astype(BF)
    for copy in v_copies:
        copy.wait()
    ladder_product(ladder_weights(v_vmem, row, [ids[n] for n in names[12:]]), pieces, lad_in, lad_ref)
    source, held, _ = lane_map(row, (256, 1), 0)
    back = jnp.where((iota((256, 240), 1) == source) & held, 1.0, 0.0).astype(BF)
    lad_out[...] = dot(lad_ref[...].astype(BF), back).astype(BF)
    o, s = iota((256, 256), 0), iota((256, 256), 1)
    target = jnp.zeros((256, 256), jnp.int32)
    for k, name in enumerate(names):
        target = jnp.where(s // 16 == k, ids[name], target)
    target = ((s % 16) // 2) * 32 + target * 2 + s % 2
    spread = jnp.where(o == target, 1.0, 0.0).astype(BF)
    for g in range(4):
        block = jnp.concatenate([c_ref[pl.ds(k * 64 + g * 16, 16), :] for k in range(16)], axis=0)
        n = 256 if g < 3 else 192
        cyc_out[pl.ds(g * 256, n), :] = dot(spread[0:n], block)[:, 0:480].astype(BF)


def last_products(names, pieces, b_all, lates, accs, lad):
    return pl.pallas_call(
        functools.partial(last_kernel, names),
        out_shape=(jax.ShapeDtypeStruct((1920, 240), BF), jax.ShapeDtypeStruct((960, 480), BF)),
        in_specs=[VMEM] * 4 + [ANY] * 11 + [VMEM] * 4,
        out_specs=(VMEM,) * 2,
        scratch_shapes=[
            pltpu.VMEM((32, 256, 256), BF),
            pltpu.VMEM((32, 128, 512), BF),
            pltpu.VMEM((32, 128, 512), BF),
            pltpu.VMEM((8, 8, 32, 128), BF),
            pltpu.VMEM((3, 32, 256, 128), BF),
            pltpu.VMEM((1024, 512), BF),
            pltpu.VMEM((1920, 256), F32),
            pltpu.SemaphoreType.DMA((3,)),
            pltpu.SemaphoreType.DMA((2, 4)),
            pltpu.SemaphoreType.DMA((8,)),
        ],
        compiler_params=PARAMS,
        cost_estimate=cost(9 * 10**9, 26 * 10**6),
        name="last",
    )(*pieces, *b_all, *lates, *accs, lad)


def permute(value, move):
    pairs = []
    for row in range(8):
        for col in range(16):
            x, y, z, core = move(row // 2, (row % 2) * 2 + (col // 2) % 2, col // 4, col % 2)
            x, y, z = x % 4, y % 4, z % 4
            pairs.append((row * 16 + col, (x * 2 + y // 2) * 16 + z * 4 + (y % 2) * 2 + core))
    return lax.ppermute(value, ("row", "col"), pairs)


KINDS = {
    "z": lambda x, y, z, c: (x, y, z + 1 - 2 * c, c),
    "x": lambda x, y, z, c: (x + 1 - 2 * c, y, z, c),
    "near": lambda x, y, z, c: (x, y ^ 1, z, c),
    "far": lambda x, y, z, c: (x, y + 2, z, c),
    "swap": lambda x, y, z, c: (x, y, z, 1 - c),
}

AHEAD = 5

MOVES = (
    ("s_b", "swap", "b"),
    ("bq", "far", "b"),
    ("d1", "x", "b"),
    ("s_a", "swap", "a"),
    ("d2", "x", "s_b"),
    ("c1", "z", "a"),
    ("s_bq", "swap", "bq"),
    ("aq", "near", "a"),
    ("c2", "z", "s_a"),
    ("d5", "x", "d1"),
    ("dq1", "x", "bq"),
    ("c5", "z", "c1"),
    ("cq1", "z", "aq"),
    ("s_d2", "swap", "d2"),
    ("s_aq", "swap", "aq"),
    ("s_c1", "swap", "c1"),
    ("dq2", "x", "s_bq"),
    ("cq5", "z", "cq1"),
    ("s_c5", "swap", "c5"),
    ("dq5", "x", "dq1"),
    ("P1", "kernel", 1),
    ("s_cq1", "swap", "cq1"),
    ("cq2", "z", "s_aq"),
    ("P0", "kernel", 0),
    ("s_dq2", "swap", "dq2"),
    ("P2", "kernel", 2),
    ("s_cq2", "swap", "cq2"),
    ("s_cq5", "swap", "cq5"),
    ("s_c2", "swap", "c2"),
)

SETS = (
    ("a", "s_a", "c1", "aq"),
    ("c2", "c5", "cq1", "s_aq"),
    ("s_c1", "cq5", "s_c5", "s_cq1"),
    ("cq2", "s_cq2", "s_cq5", "s_c2"),
)

B_NAMES = ("b", "d1", "s_d2", "d5", "bq", "dq1", "s_dq2", "dq5")

GATES = {"s_cq1": ("P1",), "s_dq2": ("P0",), "s_cq2": ("P2",)}


def on_device(amplitudes, pp_integrals, cycle_integrals, occ_map, vir_map):
    amp = jnp.transpose(amplitudes, (0, 2, 1)).reshape(1920, 240)
    have = {
        "b": prepare_b(cycle_integrals.reshape(960, 480), pp_integrals.T),
        "a": prepare(occ_map, vir_map, amp),
    }
    parts = {}

    def partial(k):
        parts[k] = partial_products(SETS[k][0], [have[n] for n in SETS[k]], [have[n] for n in B_NAMES[:4]])

    order = []
    for name, kind, source in MOVES:
        if kind == "kernel":
            partial(source)
            have[name] = parts[source][1]
            continue
        value = have[source]
        gates = [have[order[-AHEAD]]] if len(order) >= AHEAD else []
        gates += [have[g] for g in GATES.get(name, ())]
        if gates:
            value = lax.optimization_barrier((value, *gates))[0]
        with jax.named_scope(name):
            have[name] = permute(value, KINDS[kind])
        order.append(name)
    for k in range(3):
        if k not in parts:
            partial(k)
    b_all = [have[n] for n in B_NAMES]
    names = sum(SETS, ())
    lad = ladder_part(names[:12], [have[n] for n in names[:12]], b_all)
    lates, accs = [parts[k][0] for k in range(3)], [parts[k][1] for k in range(3)]
    ladder, cycle_out = last_products(names, [have[n] for n in SETS[3]], b_all, lates, accs, lad)
    ladder = jnp.transpose(ladder.reshape(30, 64, 240), (0, 2, 1))
    return ladder, cycle_out.reshape(30, 32, 480)


def solution(mesh):
    in_specs = (P("row", None, "col"), P("row", "col"), P("row", None, "col"), P(), P())
    out_specs = (P("row", None, "col"), P("row", None, "col"))
    return jax.shard_map(
        on_device, mesh=mesh, in_specs=in_specs, out_specs=out_specs, check_vma=False
    )
```

```python
import functools

import jax
import jax.numpy as jnp
from jax import lax
from jax.experimental import pallas as pl
from jax.experimental.pallas import tpu as pltpu
from jax.sharding import PartitionSpec as P

BF = jnp.bfloat16
F32 = jnp.float32
PARAMS = pltpu.CompilerParams(vmem_limit_bytes=16 * 1024 * 1024)
LAST_PARAMS = pltpu.CompilerParams(vmem_limit_bytes=16 * 1024 * 1024)
VMEM = pl.BlockSpec(memory_space=pltpu.VMEM)
SMEM = pl.BlockSpec(memory_space=pltpu.SMEM)


def cost(flops, size):
    return pl.CostEstimate(flops=flops, bytes_accessed=size, transcendentals=0)


def dot(a, b):
    return jnp.dot(a, b, preferred_element_type=F32)


def iota(shape, dim):
    return lax.broadcasted_iota(jnp.int32, shape, dim)


def here():
    return lax.axis_index("row"), lax.axis_index("col")


def slot_rows(row, col):
    x, yh, e = row // 2, row % 2, 2 * (col % 2) - 1
    return [((x + dx + 4) % 4) * 2 + (yh + dy) % 2 for dy in (0, 1) for dx in (0, e, -e, 2)]


def piece_ids(col):
    z, yl, core = col // 4, (col // 2) % 2, col % 2
    e = 2 * core - 1
    near = dict(a=(0, 0), s_a=(0, 1), c1=(e, 0), c2=(e, 1), c5=(2, 0), s_c1=(-e, 1), s_c2=(-e, 0), s_c5=(2, 1))
    far = dict(aq="a", s_aq="s_a", cq1="c1", cq2="c2", cq5="c5", s_cq1="s_c1", s_cq2="s_c2", s_cq5="s_c5")
    ids = {}
    for dy in (0, 1):
        for name in far if dy else near:
            dz, dc = near[far[name] if dy else name]
            ids[name] = ((z + dz + 4) % 4) * 4 + ((yl + dy) % 2) * 2 + (core + dc) % 2
    return ids


def lane_map(row, col, shape, dim):
    lane = iota(shape, dim)
    block, t = lane // 32, lane % 32
    start = jnp.zeros(shape, jnp.int32)
    for k, r in enumerate(slot_rows(row, col)):
        start = jnp.where(block == k, r * 30, start)
    return start + t, t < 30, block


def regroup_matrix():
    o, s = iota((256, 256), 0), iota((256, 256), 1)
    return jnp.where((s % 32 == o // 8) & (s // 32 == o % 8), 1.0, 0.0)


def place_matrix(occ_ref, row, col):
    source, held, block = lane_map(row, col, (1, 256), 1)
    keep = jnp.zeros((1, 256), jnp.int32)
    for k, r in enumerate(slot_rows(row, col)):
        keep = jnp.where(block == k, occ_ref[row, r], keep)
    keep = jnp.where(held, keep, 0)
    return jnp.where(iota((240, 256), 0) == source, keep, 0).astype(F32).astype(BF)


def screened(perm, vir_ref, piece):
    k = iota((16, 256), 0)
    value = jnp.zeros((16, 256), jnp.int32)
    for n in range(16):
        value = jnp.where(k == n, vir_ref[piece, n], value)
    spread = jnp.where(iota((256, 16), 0) // 16 == iota((256, 16), 1), 1.0, 0.0).astype(BF)
    return (perm * dot(spread, value.astype(F32).astype(BF))).astype(BF)


def regroup(perm, source, count, width, place=None):
    for first in range(0, count, 16):
        halves = []
        for m in (first, first + 8):
            n = min(count - m, 8) * 32
            if place is None:
                value = source[pl.ds(m * 32, n), :]
            else:
                value = dot(source[pl.ds(m // 2, n // 64)].reshape(n, 240), place).astype(BF)
            halves.append(dot(perm[:, 0:n], value).reshape(32, 8, width))
        yield first, jnp.concatenate(halves, axis=1).astype(BF)


def regroup_pieces(occ_ref, vir_ref, names, pieces, out):
    row, col = here()
    ids = piece_ids(col)
    perm, place = regroup_matrix(), place_matrix(occ_ref, row, col)
    for n, piece in enumerate(pieces):
        own = screened(perm, vir_ref, ids[names[n]])
        for m, part in regroup(own, piece, 60, 256, place):
            out[:, pl.ds(n * 64 + m, 16), :] = part


def regroup_kernel(names, occ_ref, vir_ref, p0, p1, p2, p3, out_ref):
    regroup_pieces(occ_ref, vir_ref, names, (p0, p1, p2, p3), out_ref)


def regroup_set(names, maps, pieces):
    return pl.pallas_call(
        functools.partial(regroup_kernel, names),
        out_shape=jax.ShapeDtypeStruct((32, 256, 256), BF),
        in_specs=[SMEM] * 2 + [VMEM] * 4,
        out_specs=VMEM,
        compiler_params=PARAMS,
        cost_estimate=cost(2 * 10**9, 8 * 10**6),
        name="regroup_" + names[0],
    )(*maps, *pieces)


def prepare_b_kernel(cyc_ref, pp_ref, out_ref):
    for first, part in regroup(regroup_matrix().astype(BF), cyc_ref, 30, 480):
        out_ref[:, pl.ds(first, 16), 0:480] = part
    for q in range(4):
        out_ref[pl.ds(2 * q, 2), :, 480:512] = pp_ref[:, q * 32:(q + 1) * 32].reshape(2, 32, 32)
    out_ref[8:32, :, 480:512] = jnp.zeros((24, 32, 32), BF)


def prepare_b(cyc, pp_t):
    return pl.pallas_call(
        prepare_b_kernel,
        out_shape=jax.ShapeDtypeStruct((32, 32, 512), BF),
        in_specs=[VMEM] * 2,
        out_specs=VMEM,
        compiler_params=PARAMS,
        cost_estimate=cost(2 * 10**8, 2 * 10**6),
        name="prepare_b",
    )(cyc, pp_t)


def slot_of(row, col, other):
    dx = (other // 2 - row // 2 + 4) % 4
    core = col % 2
    base = jnp.where(dx == 0, 0, jnp.where(dx == 3, 1 + core, jnp.where(dx == 1, 2 - core, 3)))
    return base + 4 * ((other + row) % 2)


def cycle_product(left, right, start=None):
    total = start
    for c in range(0, 32, 16):
        l = jnp.concatenate([left(c + d) for d in range(16)], axis=1)
        r = jnp.concatenate([piece[c + d] for d in range(16) for piece in right], axis=0)
        value = dot(l, r)
        total = value if total is None else total + value
    return total


def ladder_weights(v_ref, vir_ref, row, col, ids):
    s, d = iota((128, 128), 0), iota((128, 128), 1)
    lane = iota((1, 128), 1)
    tiles = []
    for pair in range(0, len(ids), 2):
        tile = jnp.zeros((64, 128), F32)
        keep = jnp.zeros((1, 128), jnp.int32)
        for half in range(2):
            p = ids[pair + half]
            slot = slot_of(row, col, p // 2)
            for a in range(2):
                values = v_ref[slot, pl.ds((p % 2) * 4 + a * 2, 2), :, :].reshape(64, 128)
                move = jnp.where((s >= 96) & (d == s - 96 + half * 64 + a * 32), 1.0, 0.0).astype(BF)
                tile = tile + dot(values, move)
            for k in range(16):
                keep = jnp.where((lane // 64 == half) & ((lane % 32) // 2 == k), vir_ref[p, k], keep)
        tiles.append((tile * keep.astype(F32)).astype(BF))
    return jnp.concatenate(tiles, axis=1)


def last_kernel(names, occ_ref, vir_ref, *refs):
    refs = list(refs)

    def take(n):
        out = refs[:n]
        del refs[:n]
        return out

    pieces, b_refs, sets, (lad_out, cyc_out, v_ref, set_ref, c_ref) = take(16), take(8), take(3), refs
    row, col = here()
    ids = piece_ids(col)
    regroup_pieces(occ_ref, vir_ref, names[12:], pieces[12:], set_ref)
    for k, part in enumerate(sets + [set_ref]):
        total = cycle_product(lambda c: part[c, :, 0:128], b_refs[0:4])
        total = cycle_product(lambda c: part[c, :, 128:256], b_refs[4:8], total)
        c_ref[pl.ds(k * 256, 256), :] = total.astype(BF)
    for k in range(8):
        v_ref[k] = b_refs[k][0:8, :, 384:512]
    weights = ladder_weights(v_ref, vir_ref, row, col, [ids[n] for n in names])
    tile = iota((1, 240), 1) // 30
    keep = jnp.zeros((1, 240), jnp.int32)
    for r in range(8):
        keep = jnp.where(tile == r, occ_ref[row, r], keep)
    keep = keep.astype(F32)

    def step(i, _):
        right = jnp.concatenate([p[i] for p in pieces], axis=0)
        lad_out[i] = (dot(weights, right) * keep).astype(BF)
        return 0

    lax.fori_loop(0, 30, step, 0, unroll=3)
    o, s = iota((256, 256), 0), iota((256, 256), 1)
    target = jnp.zeros((256, 256), jnp.int32)
    for k, name in enumerate(names):
        target = jnp.where(s // 16 == k, ids[name], target)
    target = ((s % 16) // 2) * 32 + target * 2 + s % 2
    spread = jnp.where(o == target, 1.0, 0.0).astype(BF)
    for g in range(4):
        block = jnp.concatenate([c_ref[pl.ds(k * 64 + g * 16, 16), :] for k in range(16)], axis=0)
        n = 256 if g < 3 else 192
        cyc_out[pl.ds(g * 256, n), :] = dot(spread[0:n], block)[:, 0:480].astype(BF)


def last_products(names, maps, pieces, b_all, sets):
    return pl.pallas_call(
        functools.partial(last_kernel, names),
        out_shape=(jax.ShapeDtypeStruct((30, 64, 240), BF), jax.ShapeDtypeStruct((960, 480), BF)),
        in_specs=[SMEM] * 2 + [VMEM] * 27,
        out_specs=(VMEM,) * 2,
        scratch_shapes=[
            pltpu.VMEM((8, 8, 32, 128), BF),
            pltpu.VMEM((32, 256, 256), BF),
            pltpu.VMEM((1024, 512), BF),
        ],
        compiler_params=LAST_PARAMS,
        cost_estimate=cost(12 * 10**9, 38 * 10**6),
        name="last",
    )(*maps, *pieces, *b_all, *sets)


def permute(value, move):
    pairs = []
    for row in range(8):
        for col in range(16):
            x, y, z, core = move(row // 2, (row % 2) * 2 + (col // 2) % 2, col // 4, col % 2)
            x, y, z = x % 4, y % 4, z % 4
            pairs.append((row * 16 + col, (x * 2 + y // 2) * 16 + z * 4 + (y % 2) * 2 + core))
    return lax.ppermute(value, ("row", "col"), pairs)


KINDS = {
    "z": lambda x, y, z, c: (x, y, z + 1 - 2 * c, c),
    "x": lambda x, y, z, c: (x + 1 - 2 * c, y, z, c),
    "near": lambda x, y, z, c: (x, y ^ 1, z, c),
    "far": lambda x, y, z, c: (x, y + 2, z, c),
    "swap": lambda x, y, z, c: (x, y, z, 1 - c),
}

AHEAD = 5

MOVES = (
    ("s_b", "swap", "b"),
    ("s_a", "swap", "a"),
    ("c1", "z", "a"),
    ("aq", "near", "a"),
    ("c2", "z", "s_a"),
    ("d1", "x", "b"),
    ("c5", "z", "c1"),
    ("bq", "far", "b"),
    ("d2", "x", "s_b"),
    ("P0", "kernel", 0),
    ("s_aq", "swap", "aq"),
    ("cq1", "z", "aq"),
    ("d5", "x", "d1"),
    ("s_bq", "swap", "bq"),
    ("s_c5", "swap", "c5"),
    ("dq1", "x", "bq"),
    ("s_cq1", "swap", "cq1"),
    ("cq2", "z", "s_aq"),
    ("s_c1", "swap", "c1"),
    ("P1", "kernel", 1),
    ("dq2", "x", "s_bq"),
    ("s_cq2", "swap", "cq2"),
    ("cq5", "z", "cq1"),
    ("s_d2", "swap", "d2"),
    ("dq5", "x", "dq1"),
    ("P2", "kernel", 2),
    ("s_dq2", "swap", "dq2"),
    ("s_cq5", "swap", "cq5"),
    ("s_c2", "swap", "c2"),
)

SETS = (
    ("a", "s_a", "c1", "aq"),
    ("c2", "c5", "s_aq", "cq1"),
    ("s_c5", "s_cq1", "cq2", "s_c1"),
    ("s_cq2", "cq5", "s_cq5", "s_c2"),
)

B_NAMES = ("b", "d1", "s_d2", "d5", "bq", "dq1", "s_dq2", "dq5")

GATES = {"s_aq": ("P0",), "dq2": ("P1",), "s_dq2": ("P2",)}


def on_device(amplitudes, pp_integrals, cycle_integrals, occ_map, vir_map):
    maps = (occ_map, vir_map)
    have = {
        "a": jnp.transpose(amplitudes, (0, 2, 1)),
        "b": prepare_b(cycle_integrals.reshape(960, 480), pp_integrals.T),
    }
    names = sum(SETS, ())
    sets = {}
    order = []
    for name, kind, source in MOVES:
        if kind == "kernel":
            have[name] = sets[source] = regroup_set(SETS[source], maps, [have[n] for n in SETS[source]])
            continue
        value = have[source]
        gates = [have[order[-AHEAD]]] if len(order) >= AHEAD else []
        gates += [have[g] for g in GATES.get(name, ())]
        if gates:
            value = lax.optimization_barrier((value, *gates))[0]
        with jax.named_scope(name):
            have[name] = permute(value, KINDS[kind])
        order.append(name)
    ladder, cycle_out = last_products(
        names, maps, [have[n] for n in names], [have[n] for n in B_NAMES], [sets[k] for k in range(3)]
    )
    ladder = jnp.transpose(ladder, (0, 2, 1))
    return ladder, cycle_out.reshape(30, 32, 480)


def solution(mesh):
    in_specs = (P("row", None, "col"), P("row", "col"), P("row", None, "col"), P(), P())
    out_specs = (P("row", None, "col"), P("row", None, "col"))
    return jax.shard_map(
        on_device, mesh=mesh, in_specs=in_specs, out_specs=out_specs, check_vma=False
    )
```

```python
import functools

import jax
import jax.numpy as jnp
from jax import lax
from jax.experimental import pallas as pl
from jax.experimental.pallas import tpu as pltpu
from jax.sharding import PartitionSpec as P

BF = jnp.bfloat16
F32 = jnp.float32
PARAMS = pltpu.CompilerParams(vmem_limit_bytes=7 * 1024 * 1024)
VMEM = pl.BlockSpec(memory_space=pltpu.VMEM)
SMEM = pl.BlockSpec(memory_space=pltpu.SMEM)


def cost(flops, size):
    return pl.CostEstimate(flops=flops, bytes_accessed=size, transcendentals=0)


def dot(a, b):
    return jnp.dot(a, b, preferred_element_type=F32)


def iota(shape, dim):
    return lax.broadcasted_iota(jnp.int32, shape, dim)


def here():
    return lax.axis_index("row"), lax.axis_index("col")


def slot_rows(row, col):
    x, yh, e = row // 2, row % 2, 2 * (col % 2) - 1
    return [((x + dx + 4) % 4) * 2 + (yh + dy) % 2 for dy in (0, 1) for dx in (0, e, -e, 2)]


def piece_ids(col):
    z, yl, core = col // 4, (col // 2) % 2, col % 2
    e = 2 * core - 1
    near = dict(a=(0, 0), s_a=(0, 1), c1=(e, 0), c2=(e, 1), c5=(2, 0), s_c1=(-e, 1), s_c2=(-e, 0), s_c5=(2, 1))
    far = dict(aq="a", s_aq="s_a", cq1="c1", cq2="c2", cq5="c5", s_cq1="s_c1", s_cq2="s_c2", s_cq5="s_c5")
    ids = {}
    for dy in (0, 1):
        for name in far if dy else near:
            dz, dc = near[far[name] if dy else name]
            ids[name] = ((z + dz + 4) % 4) * 4 + ((yl + dy) % 2) * 2 + (core + dc) % 2
    return ids


def lane_map(row, col, shape, dim):
    lane = iota(shape, dim)
    block, t = lane // 32, lane % 32
    start = jnp.zeros(shape, jnp.int32)
    for k, r in enumerate(slot_rows(row, col)):
        start = jnp.where(block == k, r * 30, start)
    return start + t, t < 30, block


def regroup_matrix():
    o, s = iota((256, 256), 0), iota((256, 256), 1)
    return jnp.where((s % 32 == o // 8) & (s // 32 == o % 8), 1.0, 0.0)


def place_matrix(occ_ref, row, col):
    source, held, block = lane_map(row, col, (1, 256), 1)
    keep = jnp.zeros((1, 256), jnp.int32)
    for k, r in enumerate(slot_rows(row, col)):
        keep = jnp.where(block == k, occ_ref[row, r], keep)
    keep = jnp.where(held, keep, 0)
    return jnp.where(iota((240, 256), 0) == source, keep, 0).astype(F32).astype(BF)


def screened(perm, vir_ref, piece):
    k = iota((16, 256), 0)
    value = jnp.zeros((16, 256), jnp.int32)
    for n in range(16):
        value = jnp.where(k == n, vir_ref[piece, n], value)
    spread = jnp.where(iota((256, 16), 0) // 16 == iota((256, 16), 1), 1.0, 0.0).astype(BF)
    return (perm * dot(spread, value.astype(F32).astype(BF))).astype(BF)


def regroup(perm, source, count, width, place=None):
    for first in range(0, count, 16):
        halves = []
        for m in (first, first + 8):
            n = min(count - m, 8) * 32
            if place is None:
                value = source[pl.ds(m * 32, n), :]
            else:
                value = dot(source[pl.ds(m // 2, n // 64)].reshape(n, 240), place).astype(BF)
            halves.append(dot(perm[:, 0:n], value).reshape(32, 8, width))
        yield first, jnp.concatenate(halves, axis=1).astype(BF)


def regroup_pieces(occ_ref, vir_ref, names, pieces, out):
    row, col = here()
    ids = piece_ids(col)
    perm, place = regroup_matrix(), place_matrix(occ_ref, row, col)
    for n, piece in enumerate(pieces):
        own = screened(perm, vir_ref, ids[names[n]])
        for m, part in regroup(own, piece, 60, 256, place):
            out[:, pl.ds(n * 64 + m, 16), :] = part


def regroup_kernel(names, occ_ref, vir_ref, p0, p1, p2, p3, out_ref):
    regroup_pieces(occ_ref, vir_ref, names, (p0, p1, p2, p3), out_ref)


def regroup_set(names, maps, pieces):
    return pl.pallas_call(
        functools.partial(regroup_kernel, names),
        out_shape=jax.ShapeDtypeStruct((32, 256, 256), BF),
        in_specs=[SMEM] * 2 + [VMEM] * 4,
        out_specs=VMEM,
        compiler_params=PARAMS,
        cost_estimate=cost(1000, 1000),
        name="regroup_" + names[0],
    )(*maps, *pieces)


def prepare_b_kernel(cyc_ref, pp_ref, out_ref):
    for first, part in regroup(regroup_matrix().astype(BF), cyc_ref, 30, 480):
        out_ref[:, pl.ds(first, 16), 0:480] = part
    for q in range(4):
        out_ref[pl.ds(2 * q, 2), :, 480:512] = pp_ref[:, q * 32:(q + 1) * 32].reshape(2, 32, 32)
    out_ref[8:32, :, 480:512] = jnp.zeros((24, 32, 32), BF)


def prepare_b(cyc, pp_t):
    return pl.pallas_call(
        prepare_b_kernel,
        out_shape=jax.ShapeDtypeStruct((32, 32, 512), BF),
        in_specs=[VMEM] * 2,
        out_specs=VMEM,
        compiler_params=PARAMS,
        cost_estimate=cost(2 * 10**8, 2 * 10**6),
        name="prepare_b",
    )(cyc, pp_t)


def slot_of(row, col, other):
    dx = (other // 2 - row // 2 + 4) % 4
    core = col % 2
    base = jnp.where(dx == 0, 0, jnp.where(dx == 3, 1 + core, jnp.where(dx == 1, 2 - core, 3)))
    return base + 4 * ((other + row) % 2)


def cycle_product(left, right, start=None):
    total = start
    for c in range(0, 32, 16):
        l = jnp.concatenate([left(c + d) for d in range(16)], axis=1)
        r = jnp.concatenate([piece[c + d] for d in range(16) for piece in right], axis=0)
        value = dot(l, r)
        total = value if total is None else total + value
    return total


def ladder_weights(v_ref, vir_ref, row, col, ids):
    s, d = iota((128, 128), 0), iota((128, 128), 1)
    lane = iota((1, 128), 1)
    tiles = []
    for pair in range(0, len(ids), 2):
        tile = jnp.zeros((64, 128), F32)
        keep = jnp.zeros((1, 128), jnp.int32)
        for half in range(2):
            p = ids[pair + half]
            slot = slot_of(row, col, p // 2)
            for a in range(2):
                values = v_ref[slot, pl.ds((p % 2) * 4 + a * 2, 2), :, :].reshape(64, 128)
                move = jnp.where((s >= 96) & (d == s - 96 + half * 64 + a * 32), 1.0, 0.0).astype(BF)
                tile = tile + dot(values, move)
            for k in range(16):
                keep = jnp.where((lane // 64 == half) & ((lane % 32) // 2 == k), vir_ref[p, k], keep)
        tiles.append((tile * keep.astype(F32)).astype(BF))
    return jnp.concatenate(tiles, axis=1)


def early_kernel(*refs):
    sets, b_refs, out_ref = refs[:3], refs[3:7], refs[7]
    for k, part in enumerate(sets):
        out_ref[pl.ds(k * 256, 256), :] = cycle_product(lambda c: part[c, :, 0:128], b_refs)


def early_products(sets, b_early):
    return pl.pallas_call(
        early_kernel,
        out_shape=jax.ShapeDtypeStruct((768, 512), F32),
        in_specs=[VMEM] * 7,
        out_specs=VMEM,
        compiler_params=PARAMS,
        cost_estimate=cost(1000, 1000),
        name="early",
    )(*sets, *b_early)


def last_kernel(names, occ_ref, vir_ref, *refs):
    pieces, b_refs, sets, refs = refs[:16], refs[16:24], refs[24:28], refs[28:]
    start_ref, lad_out, cyc_out, v_ref, c_ref = refs
    row, col = here()
    ids = piece_ids(col)
    for k, part in enumerate(sets):
        at = pl.ds(k * 256, 256)
        start = start_ref[at, :] if k < 3 else cycle_product(lambda c: part[c, :, 0:128], b_refs[0:4])
        c_ref[at, :] = cycle_product(lambda c: part[c, :, 128:256], b_refs[4:8], start).astype(BF)
    for k in range(8):
        v_ref[k] = b_refs[k][0:8, :, 384:512]
    weights = ladder_weights(v_ref, vir_ref, row, col, [ids[n] for n in names])
    tile = iota((1, 240), 1) // 30
    keep = jnp.zeros((1, 240), jnp.int32)
    for r in range(8):
        keep = jnp.where(tile == r, occ_ref[row, r], keep)
    keep = keep.astype(F32)

    def step(i, _):
        right = jnp.concatenate([p[i] for p in pieces], axis=0)
        lad_out[i] = (dot(weights, right) * keep).astype(BF)
        return 0

    lax.fori_loop(0, 30, step, 0, unroll=3)
    o, s = iota((256, 256), 0), iota((256, 256), 1)
    target = jnp.zeros((256, 256), jnp.int32)
    for k, name in enumerate(names):
        target = jnp.where(s // 16 == k, ids[name], target)
    target = ((s % 16) // 2) * 32 + target * 2 + s % 2
    spread = jnp.where(o == target, 1.0, 0.0).astype(BF)
    for g in range(4):
        block = jnp.concatenate([c_ref[pl.ds(k * 64 + g * 16, 16), :] for k in range(16)], axis=0)
        n = 256 if g < 3 else 192
        cyc_out[pl.ds(g * 256, n), :] = dot(spread[0:n], block)[:, 0:480].astype(BF)


def last_products(names, maps, pieces, b_all, sets, start):
    return pl.pallas_call(
        functools.partial(last_kernel, names),
        out_shape=(jax.ShapeDtypeStruct((30, 64, 240), BF), jax.ShapeDtypeStruct((960, 480), BF)),
        in_specs=[SMEM] * 2 + [VMEM] * 29,
        out_specs=(VMEM,) * 2,
        scratch_shapes=[
            pltpu.VMEM((8, 8, 32, 128), BF),
            pltpu.VMEM((1024, 512), BF),
        ],
        compiler_params=PARAMS,
        cost_estimate=cost(12 * 10**9, 38 * 10**6),
        name="last",
    )(*maps, *pieces, *b_all, *sets, start)


def permute(value, move):
    pairs = []
    for row in range(8):
        for col in range(16):
            x, y, z, core = move(row // 2, (row % 2) * 2 + (col // 2) % 2, col // 4, col % 2)
            x, y, z = x % 4, y % 4, z % 4
            pairs.append((row * 16 + col, (x * 2 + y // 2) * 16 + z * 4 + (y % 2) * 2 + core))
    return lax.ppermute(value, ("row", "col"), pairs)


KINDS = {
    "z": lambda x, y, z, c: (x, y, z + 1 - 2 * c, c),
    "x": lambda x, y, z, c: (x + 1 - 2 * c, y, z, c),
    "near": lambda x, y, z, c: (x, y ^ 1, z, c),
    "far": lambda x, y, z, c: (x, y + 2, z, c),
    "swap": lambda x, y, z, c: (x, y, z, 1 - c),
}

AHEAD = 5

MOVES = (
    ("s_b", "swap", "b"),
    ("s_a", "swap", "a"),
    ("c1", "z", "a"),
    ("aq", "near", "a"),
    ("c2", "z", "s_a"),
    ("d1", "x", "b"),
    ("c5", "z", "c1"),
    ("bq", "far", "b"),
    ("d2", "x", "s_b"),
    ("P0", "kernel", 0),
    ("s_aq", "swap", "aq"),
    ("cq1", "z", "aq"),
    ("d5", "x", "d1"),
    ("s_bq", "swap", "bq"),
    ("s_c5", "swap", "c5"),
    ("dq1", "x", "bq"),
    ("s_cq1", "swap", "cq1"),
    ("cq2", "z", "s_aq"),
    ("s_c1", "swap", "c1"),
    ("P1", "kernel", 1),
    ("dq2", "x", "s_bq"),
    ("s_cq2", "swap", "cq2"),
    ("cq5", "z", "cq1"),
    ("s_d2", "swap", "d2"),
    ("dq5", "x", "dq1"),
    ("P2", "kernel", 2),
    ("s_dq2", "swap", "dq2"),
    ("s_cq5", "swap", "cq5"),
    ("s_c2", "swap", "c2"),
)

SETS = (
    ("a", "s_a", "c1", "aq"),
    ("c2", "c5", "s_aq", "cq1"),
    ("s_c5", "s_cq1", "cq2", "s_c1"),
    ("s_cq2", "cq5", "s_cq5", "s_c2"),
)

B_NAMES = ("b", "d1", "s_d2", "d5", "bq", "dq1", "s_dq2", "dq5")

GATES = {"s_aq": ("P0",), "dq2": ("P1",), "s_dq2": ("P2",)}


def on_device(amplitudes, pp_integrals, cycle_integrals, occ_map, vir_map):
    maps = (occ_map, vir_map)
    have = {
        "a": jnp.transpose(amplitudes, (0, 2, 1)),
        "b": prepare_b(cycle_integrals.reshape(960, 480), pp_integrals.T),
    }
    names = sum(SETS, ())
    sets = {}
    order = []
    for name, kind, source in MOVES:
        if kind == "kernel":
            have[name] = sets[source] = regroup_set(SETS[source], maps, [have[n] for n in SETS[source]])
            continue
        value = have[source]
        gates = [have[order[-AHEAD]]] if len(order) >= AHEAD else []
        gates += [have[g] for g in GATES.get(name, ())]
        if gates:
            value = lax.optimization_barrier((value, *gates))[0]
        with jax.named_scope(name):
            have[name] = permute(value, KINDS[kind])
        order.append(name)
    sets[3] = regroup_set(SETS[3], maps, [have[n] for n in SETS[3]])
    sets, b_all = [sets[k] for k in range(4)], [have[n] for n in B_NAMES]
    start = early_products(sets[:3], b_all[:4])
    ladder, cycle_out = last_products(names, maps, [have[n] for n in names], b_all, sets, start)
    ladder = jnp.transpose(ladder, (0, 2, 1))
    return ladder, cycle_out.reshape(30, 32, 480)


def solution(mesh):
    in_specs = (P("row", None, "col"), P("row", "col"), P("row", None, "col"), P(), P())
    out_specs = (P("row", None, "col"), P("row", None, "col"))
    return jax.shard_map(
        on_device, mesh=mesh, in_specs=in_specs, out_specs=out_specs, check_vma=False
    )
```

```python
import functools

import jax
import jax.numpy as jnp
from jax import lax
from jax.experimental import pallas as pl
from jax.experimental.pallas import tpu as pltpu
from jax.sharding import PartitionSpec as P

BF = jnp.bfloat16
F32 = jnp.float32
PARAMS = pltpu.CompilerParams(vmem_limit_bytes=7 * 1024 * 1024)
VMEM = pl.BlockSpec(memory_space=pltpu.VMEM)
SMEM = pl.BlockSpec(memory_space=pltpu.SMEM)


def cost(flops, size):
    return pl.CostEstimate(flops=flops, bytes_accessed=size, transcendentals=0)


def dot(a, b):
    return jnp.dot(a, b, preferred_element_type=F32)


def iota(shape, dim):
    return lax.broadcasted_iota(jnp.int32, shape, dim)


def here():
    return lax.axis_index("row"), lax.axis_index("col")


def slot_rows(row, col):
    x, yh, e = row // 2, row % 2, 2 * (col % 2) - 1
    return [((x + dx + 4) % 4) * 2 + (yh + dy) % 2 for dy in (0, 1) for dx in (0, e, -e, 2)]


def piece_ids(col):
    z, yl, core = col // 4, (col // 2) % 2, col % 2
    e = 2 * core - 1
    near = dict(a=(0, 0), s_a=(0, 1), c1=(e, 0), c2=(e, 1), c5=(2, 0), s_c1=(-e, 1), s_c2=(-e, 0), s_c5=(2, 1))
    far = dict(aq="a", s_aq="s_a", cq1="c1", cq2="c2", cq5="c5", s_cq1="s_c1", s_cq2="s_c2", s_cq5="s_c5")
    ids = {}
    for dy in (0, 1):
        for name in far if dy else near:
            dz, dc = near[far[name] if dy else name]
            ids[name] = ((z + dz + 4) % 4) * 4 + ((yl + dy) % 2) * 2 + (core + dc) % 2
    return ids


def lane_map(row, col, shape, dim):
    lane = iota(shape, dim)
    block, t = lane // 32, lane % 32
    start = jnp.zeros(shape, jnp.int32)
    for k, r in enumerate(slot_rows(row, col)):
        start = jnp.where(block == k, r * 30, start)
    return start + t, t < 30, block


def regroup_matrix():
    o, s = iota((256, 256), 0), iota((256, 256), 1)
    return jnp.where((s % 32 == o // 8) & (s // 32 == o % 8), 1.0, 0.0)


def place_matrix(occ_ref, row, col):
    source, held, block = lane_map(row, col, (1, 256), 1)
    keep = jnp.zeros((1, 256), jnp.int32)
    for k, r in enumerate(slot_rows(row, col)):
        keep = jnp.where(block == k, occ_ref[row, r], keep)
    keep = jnp.where(held, keep, 0)
    return jnp.where(iota((240, 256), 0) == source, keep, 0).astype(F32).astype(BF)


def screened(perm, vir_ref, piece):
    k = iota((16, 256), 0)
    value = jnp.zeros((16, 256), jnp.int32)
    for n in range(16):
        value = jnp.where(k == n, vir_ref[piece, n], value)
    spread = jnp.where(iota((256, 16), 0) // 16 == iota((256, 16), 1), 1.0, 0.0).astype(BF)
    return (perm * dot(spread, value.astype(F32).astype(BF))).astype(BF)


def regroup(perm, source, count, width, place=None):
    for first in range(0, count, 16):
        halves = []
        for m in (first, first + 8):
            n = min(count - m, 8) * 32
            if place is None:
                value = source[pl.ds(m * 32, n), :]
            else:
                value = dot(source[pl.ds(m // 2, n // 64)].reshape(n, 240), place).astype(BF)
            halves.append(dot(perm[:, 0:n], value).reshape(32, 8, width))
        yield first, jnp.concatenate(halves, axis=1).astype(BF)


def regroup_pieces(occ_ref, vir_ref, names, pieces, out):
    row, col = here()
    ids = piece_ids(col)
    perm, place = regroup_matrix(), place_matrix(occ_ref, row, col)
    for n, piece in enumerate(pieces):
        own = screened(perm, vir_ref, ids[names[n]])
        for m, part in regroup(own, piece, 60, 256, place):
            out[:, pl.ds(n * 64 + m, 16), :] = part


def regroup_kernel(names, occ_ref, vir_ref, p0, p1, p2, p3, out_ref):
    regroup_pieces(occ_ref, vir_ref, names, (p0, p1, p2, p3), out_ref)


def regroup_set(names, maps, pieces):
    return pl.pallas_call(
        functools.partial(regroup_kernel, names),
        out_shape=jax.ShapeDtypeStruct((32, 256, 256), BF),
        in_specs=[SMEM] * 2 + [VMEM] * 4,
        out_specs=VMEM,
        compiler_params=PARAMS,
        cost_estimate=cost(1000, 1000),
        name="regroup_" + names[0],
    )(*maps, *pieces)


def prepare_b_kernel(cyc_ref, pp_ref, out_ref):
    for first, part in regroup(regroup_matrix().astype(BF), cyc_ref, 30, 480):
        out_ref[:, pl.ds(first, 16), 0:480] = part
    for q in range(4):
        out_ref[pl.ds(2 * q, 2), :, 480:512] = pp_ref[:, q * 32:(q + 1) * 32].reshape(2, 32, 32)
    out_ref[8:32, :, 480:512] = jnp.zeros((24, 32, 32), BF)


def prepare_b(cyc, pp_t):
    return pl.pallas_call(
        prepare_b_kernel,
        out_shape=jax.ShapeDtypeStruct((32, 32, 512), BF),
        in_specs=[VMEM] * 2,
        out_specs=VMEM,
        compiler_params=PARAMS,
        cost_estimate=cost(2 * 10**8, 2 * 10**6),
        name="prepare_b",
    )(cyc, pp_t)


def slot_of(row, col, other):
    dx = (other // 2 - row // 2 + 4) % 4
    core = col % 2
    base = jnp.where(dx == 0, 0, jnp.where(dx == 3, 1 + core, jnp.where(dx == 1, 2 - core, 3)))
    return base + 4 * ((other + row) % 2)


def cycle_product(left, right, start=None):
    total = start
    for c in range(0, 32, 16):
        l = jnp.concatenate([left(c + d) for d in range(16)], axis=1)
        r = jnp.concatenate([piece[c + d] for d in range(16) for piece in right], axis=0)
        value = dot(l, r)
        total = value if total is None else total + value
    return total


def ladder_weights(v_ref, vir_ref, row, col, ids):
    s, d = iota((128, 128), 0), iota((128, 128), 1)
    lane = iota((1, 128), 1)
    tiles = []
    for pair in range(0, len(ids), 2):
        tile = jnp.zeros((64, 128), F32)
        keep = jnp.zeros((1, 128), jnp.int32)
        for half in range(2):
            p = ids[pair + half]
            slot = slot_of(row, col, p // 2)
            for a in range(2):
                values = v_ref[slot, pl.ds((p % 2) * 4 + a * 2, 2), :, :].reshape(64, 128)
                move = jnp.where((s >= 96) & (d == s - 96 + half * 64 + a * 32), 1.0, 0.0).astype(BF)
                tile = tile + dot(values, move)
            for k in range(16):
                keep = jnp.where((lane // 64 == half) & ((lane % 32) // 2 == k), vir_ref[p, k], keep)
        tiles.append((tile * keep.astype(F32)).astype(BF))
    return jnp.concatenate(tiles, axis=1)


def early_kernel(*refs):
    sets, b_refs, out_ref = refs[:3], refs[3:7], refs[7]
    for k, part in enumerate(sets):
        out_ref[pl.ds(k * 256, 256), :] = cycle_product(lambda c: part[c, :, 0:128], b_refs)


def early_products(sets, b_early):
    return pl.pallas_call(
        early_kernel,
        out_shape=jax.ShapeDtypeStruct((768, 512), F32),
        in_specs=[VMEM] * 7,
        out_specs=VMEM,
        compiler_params=PARAMS,
        cost_estimate=cost(1000, 1000),
        name="early",
    )(*sets, *b_early)


def last_kernel(names, occ_ref, vir_ref, *refs):
    pieces, b_refs, sets, refs = refs[:16], refs[16:24], refs[24:28], refs[28:]
    start_ref, lad_out, cyc_out, v_ref, c_ref = refs
    row, col = here()
    ids = piece_ids(col)
    for k, part in enumerate(sets):
        at = pl.ds(k * 256, 256)
        start = start_ref[at, :] if k < 3 else cycle_product(lambda c: part[c, :, 0:128], b_refs[0:4])
        c_ref[at, :] = cycle_product(lambda c: part[c, :, 128:256], b_refs[4:8], start).astype(BF)
    for k in range(8):
        v_ref[k] = b_refs[k][0:8, :, 384:512]
    weights = ladder_weights(v_ref, vir_ref, row, col, [ids[n] for n in names])
    tile = iota((1, 240), 1) // 30
    keep = jnp.zeros((1, 240), jnp.int32)
    for r in range(8):
        keep = jnp.where(tile == r, occ_ref[row, r], keep)
    keep = keep.astype(F32)

    def step(i, _):
        right = jnp.concatenate([p[i] for p in pieces], axis=0)
        lad_out[i] = (dot(weights, right) * keep).astype(BF)
        return 0

    lax.fori_loop(0, 30, step, 0, unroll=10)
    o, s = iota((256, 256), 0), iota((256, 256), 1)
    target = jnp.zeros((256, 256), jnp.int32)
    for k, name in enumerate(names):
        target = jnp.where(s // 16 == k, ids[name], target)
    target = ((s % 16) // 2) * 32 + target * 2 + s % 2
    spread = jnp.where(o == target, 1.0, 0.0).astype(BF)
    for g in range(4):
        block = jnp.concatenate([c_ref[pl.ds(k * 64 + g * 16, 16), :] for k in range(16)], axis=0)
        n = 256 if g < 3 else 192
        cyc_out[pl.ds(g * 256, n), :] = dot(spread[0:n], block)[:, 0:480].astype(BF)


def last_products(names, maps, pieces, b_all, sets, start):
    return pl.pallas_call(
        functools.partial(last_kernel, names),
        out_shape=(jax.ShapeDtypeStruct((30, 64, 240), BF), jax.ShapeDtypeStruct((960, 480), BF)),
        in_specs=[SMEM] * 2 + [VMEM] * 29,
        out_specs=(VMEM,) * 2,
        scratch_shapes=[
            pltpu.VMEM((8, 8, 32, 128), BF),
            pltpu.VMEM((1024, 512), BF),
        ],
        compiler_params=PARAMS,
        cost_estimate=cost(12 * 10**9, 38 * 10**6),
        name="last",
    )(*maps, *pieces, *b_all, *sets, start)


def permute(value, move):
    pairs = []
    for row in range(8):
        for col in range(16):
            x, y, z, core = move(row // 2, (row % 2) * 2 + (col // 2) % 2, col // 4, col % 2)
            x, y, z = x % 4, y % 4, z % 4
            pairs.append((row * 16 + col, (x * 2 + y // 2) * 16 + z * 4 + (y % 2) * 2 + core))
    return lax.ppermute(value, ("row", "col"), pairs)


KINDS = {
    "z": lambda x, y, z, c: (x, y, z + 1 - 2 * c, c),
    "x": lambda x, y, z, c: (x + 1 - 2 * c, y, z, c),
    "near": lambda x, y, z, c: (x, y ^ 1, z, c),
    "far": lambda x, y, z, c: (x, y + 2, z, c),
    "swap": lambda x, y, z, c: (x, y, z, 1 - c),
}

AHEAD = 5

MOVES = (
    ("s_b", "swap", "b"),
    ("s_a", "swap", "a"),
    ("c1", "z", "a"),
    ("aq", "near", "a"),
    ("c2", "z", "s_a"),
    ("d1", "x", "b"),
    ("c5", "z", "c1"),
    ("bq", "far", "b"),
    ("d2", "x", "s_b"),
    ("P0", "kernel", 0),
    ("s_aq", "swap", "aq"),
    ("cq1", "z", "aq"),
    ("d5", "x", "d1"),
    ("s_bq", "swap", "bq"),
    ("s_c5", "swap", "c5"),
    ("dq1", "x", "bq"),
    ("s_cq1", "swap", "cq1"),
    ("cq2", "z", "s_aq"),
    ("s_c1", "swap", "c1"),
    ("P1", "kernel", 1),
    ("dq2", "x", "s_bq"),
    ("s_cq2", "swap", "cq2"),
    ("cq5", "z", "cq1"),
    ("s_d2", "swap", "d2"),
    ("dq5", "x", "dq1"),
    ("P2", "kernel", 2),
    ("s_dq2", "swap", "dq2"),
    ("s_cq5", "swap", "cq5"),
    ("s_c2", "swap", "c2"),
)

SETS = (
    ("a", "s_a", "c1", "aq"),
    ("c2", "c5", "s_aq", "cq1"),
    ("s_c5", "s_cq1", "cq2", "s_c1"),
    ("s_cq2", "cq5", "s_cq5", "s_c2"),
)

B_NAMES = ("b", "d1", "s_d2", "d5", "bq", "dq1", "s_dq2", "dq5")

GATES = {"s_aq": ("P0",), "dq2": ("P1",), "s_dq2": ("P2",)}


def on_device(amplitudes, pp_integrals, cycle_integrals, occ_map, vir_map):
    maps = (occ_map, vir_map)
    have = {
        "a": jnp.transpose(amplitudes, (0, 2, 1)),
        "b": prepare_b(cycle_integrals.reshape(960, 480), pp_integrals.T),
    }
    names = sum(SETS, ())
    sets = {}
    order = []
    for name, kind, source in MOVES:
        if kind == "kernel":
            have[name] = sets[source] = regroup_set(SETS[source], maps, [have[n] for n in SETS[source]])
            continue
        value = have[source]
        gates = [have[order[-AHEAD]]] if len(order) >= AHEAD else []
        gates += [have[g] for g in GATES.get(name, ())]
        if gates:
            value = lax.optimization_barrier((value, *gates))[0]
        with jax.named_scope(name):
            have[name] = permute(value, KINDS[kind])
        order.append(name)
    sets[3] = regroup_set(SETS[3], maps, [have[n] for n in SETS[3]])
    sets, b_all = [sets[k] for k in range(4)], [have[n] for n in B_NAMES]
    start = early_products(sets[:3], b_all[:4])
    ladder, cycle_out = last_products(names, maps, [have[n] for n in names], b_all, sets, start)
    ladder = jnp.transpose(ladder, (0, 2, 1))
    return ladder, cycle_out.reshape(30, 32, 480)


def solution(mesh):
    in_specs = (P("row", None, "col"), P("row", "col"), P("row", None, "col"), P(), P())
    out_specs = (P("row", None, "col"), P("row", None, "col"))
    return jax.shard_map(
        on_device, mesh=mesh, in_specs=in_specs, out_specs=out_specs, check_vma=False
    )
```
